32 devices in a mesh: snap: 8 (over z, y), space: 4 (over x, core).
Axes of the slice: x: 2, y: 2, z: 4, core: 2. Of those that a mesh axis runs over, the one named last changes fastest.
Arguments:
- snapshots: bfloat16 [1024, 2, 16, 720], P('snap', None, 'space'), may hold values from -6 to 6
- lon_coeff: float32 [2, 16, 720], P(None, 'space'), may hold values from 0.05 to 0.24
- lat_coeff: float32 [2, 16, 720], P(None, 'space'), may hold values from 0.1 to 0.24
Outputs:
- gram: float32 [1024, 1024], P('snap', 'space')
The draws below stay inside these ranges and needn't reach their ends.
All inputs are finite; a program needn't handle non-finite values.
Results may differ from the reference program's by a relative error of at most 0.00062.
Values may be sent and summed in bfloat16 or wider, within the bound.
No kernel may reach another device: no remote copies, remote signals or barrier semaphores. Data moves between devices by JAX's collectives and lax.ppermute only.
A program may use at most 128 MiB of HBM per device.

```python
import math
import jax
import jax.numpy as jnp
from jax import lax

FIELDS = 2
NLON = 720
NLAT = 16
SNAPS = 1024


def steps_of(own_key, dims, cuts, low, largest):
    gain, own = 1.0, jax.random.fold_in(own_key, 6)
    for axis_at, shards_of in cuts:
        draws = jnp.exp(jax.random.uniform(jax.random.fold_in(own, axis_at), (shards_of,), jnp.float32, low / len(cuts), largest / len(cuts)))
        gain = gain * jnp.repeat(draws, dims[axis_at] // shards_of).reshape([-1 if axis == axis_at else 1 for axis in range(len(dims))])
    return gain


def normal_values(stream_key, dims, width, reach, split=(), dtype=jnp.bfloat16):
    loudness = steps_of(stream_key, dims, split, -0.22, 0.18) if split else 1.0
    entries = jax.random.normal(stream_key, dims, jnp.float32) * width * loudness
    return jnp.minimum(jnp.maximum(entries, -reach), reach).astype(dtype)


def setup_inputs(seed: int = 0) -> dict:
    key_of = jax.random.split(jax.random.key(seed), 4)
    snapshots = normal_values(key_of[0], (SNAPS, FIELDS, NLAT, NLON), 1.0, 6.0, ((0, 8), (2, 4)))
    lon_coeff = jnp.clip(jnp.exp(math.log(0.24) - 1.5686159 * jax.random.uniform(key_of[1], (FIELDS, NLAT, NLON), jnp.float32) ** steps_of(key_of[1], (FIELDS, NLAT, NLON), ((1, 4),), -0.2, 0.2)), 0.05, 0.24)
    lat_coeff = jnp.clip(jnp.exp(math.log(0.24) - 0.8754687 * jax.random.uniform(key_of[2], (FIELDS, NLAT, NLON), jnp.float32) ** steps_of(key_of[2], (FIELDS, NLAT, NLON), ((1, 4),), -0.2, 0.2)), 0.1, 0.24)
    return {"snapshots": snapshots, "lon_coeff": lon_coeff, "lat_coeff": lat_coeff}


def reference(snapshots, lon_coeff, lat_coeff):
    values = snapshots.astype(jnp.float32)
    lon_part = jnp.roll(values, 1, axis=3) + jnp.roll(values, -1, axis=3) - 2.0 * values
    padded = jnp.pad(values, ((0, 0), (0, 0), (1, 1), (0, 0)))
    lat_part = padded[:, :, 2:] + padded[:, :, :-2] - 2.0 * values
    smooth = values + lon_coeff * lon_part + lat_coeff * lat_part
    rows = jnp.arange(NLAT).astype(jnp.float32)
    angle = (45.0 + 0.5 * (rows + 0.5 - NLAT / 2.0)) * (math.pi / 180.0)
    cosine = jnp.cos(angle)
    total = FIELDS * NLON * jnp.sum(cosine)
    factor = jnp.sqrt(cosine) * total ** (-0.25)
    scaled = (smooth * factor[:, None]).astype(jnp.bfloat16).reshape(smooth.shape[0], -1)
    return lax.dot_general(scaled, scaled, (((1,), (1,)), ((), ())), preferred_element_type=jnp.float32)
```

```python
import math

import jax
import jax.numpy as jnp
from jax import lax
from jax.sharding import PartitionSpec as P


def flip(cells, axis, bits):
    count = lax.axis_size(axis)
    return lax.ppermute(cells, axis, [(i, i ^ bits) for i in range(count)])


def scaled_cells(cells, lon_coeff, lat_coeff):
    fields, rows, nlon, snaps = cells.shape
    bands = lax.axis_size("space")
    ends = bands - 1
    above = lax.ppermute(cells[:, rows - 1 :], "space", [(i, i + 1) for i in range(ends)])
    below = lax.ppermute(cells[:, :1], "space", [(i + 1, i) for i in range(ends)])
    padded = jnp.concatenate([above, cells, below], axis=1).astype(jnp.float32)
    values = cells.astype(jnp.float32)
    lon_part = jnp.roll(values, 1, axis=2) + jnp.roll(values, -1, axis=2) - 2.0 * values
    lat_part = padded[:, 2:] + padded[:, :-2] - 2.0 * values
    smooth = values + lon_coeff[..., None] * lon_part + lat_coeff[..., None] * lat_part
    nlat = bands * rows
    every_row = jnp.arange(nlat).astype(jnp.float32)
    every_cos = jnp.cos((45.0 + 0.5 * (every_row + 0.5 - nlat / 2.0)) * (math.pi / 180.0))
    total = fields * nlon * jnp.sum(every_cos)
    my_rows = (lax.axis_index("space") * rows + jnp.arange(rows)).astype(jnp.float32)
    cosine = jnp.cos((45.0 + 0.5 * (my_rows + 0.5 - nlat / 2.0)) * (math.pi / 180.0))
    factor = jnp.sqrt(cosine) * total ** (-0.25)
    return (smooth * factor[:, None, None]).astype(jnp.bfloat16)


def shards(snapshots, lon_coeff, lat_coeff):
    snaps, fields, rows, nlon = snapshots.shape
    groups, bands = lax.axis_size("snap"), lax.axis_size("space")
    layers, columns = groups // 2, bands // 2
    me, band = lax.axis_index("snap"), lax.axis_index("space")
    layer, column, core = me // 2, band // 2, band % 2
    scaled = scaled_cells(jnp.transpose(snapshots, (1, 2, 3, 0)), lon_coeff, lat_coeff)
    slices = scaled.reshape(layers, -1, snaps)
    held = []
    for j in range(layers):
        mine = lax.dynamic_index_in_dim(slices, layer ^ j, 0, keepdims=False)
        held.append(flip(mine, "snap", 2 * j) if j else mine)
    other = [flip(piece, "snap", 1) for piece in held]
    stack = jnp.stack([piece for pair in zip(held, other) for piece in pair])
    stack = jnp.concatenate([stack, flip(stack, "space", 1)], axis=1)
    left = jnp.concatenate([stack[2 * j] for j in range(layers)], axis=1)
    share = groups // bands
    right = []
    for i in range(columns):
        for g in range(share):
            group = ((column ^ i) * 2 + core) * share + g
            right.append(lax.dynamic_index_in_dim(stack, group ^ me, 0, keepdims=False))
    right = jnp.concatenate(right, axis=1)
    product = lax.dot_general(
        left, right, (((0,), (0,)), ((), ())), preferred_element_type=jnp.float32
    )
    product = product.reshape(layers, snaps, columns, share * snaps)
    total = product[0, :, 0]
    for j in range(layers):
        for i in range(columns):
            if i or j:
                pairs = [
                    (s * bands + b, (s ^ (2 * j)) * bands + (b ^ (2 * i)))
                    for s in range(groups)
                    for b in range(bands)
                ]
                total += lax.ppermute(product[j, :, i], ("snap", "space"), pairs)
    return total


def solution(mesh):
    return jax.shard_map(
        shards,
        mesh=mesh,
        in_specs=(P("snap", None, "space", None), P(None, "space", None), P(None, "space", None)),
        out_specs=P("snap", "space"),
        check_vma=False,
    )
```

```python
import functools
import math

import jax
import jax.numpy as jnp
import numpy as np
from jax import lax
from jax.experimental import pallas as pl
from jax.experimental.pallas import tpu as pltpu
from jax.sharding import PartitionSpec as P

EXTRA = 8
VMEM_BYTES = 48 * 2**20


def flip(cells, axis, bits):
    count = lax.axis_size(axis)
    return lax.ppermute(cells, axis, [(i, i ^ bits) for i in range(count)])


def after(value, *earlier):
    return lax.optimization_barrier((value, *earlier))[0]


def row_factors(nlat, fields, nlon):
    cosine = np.cos(np.deg2rad(45.0 + 0.5 * (np.arange(nlat) + 0.5 - nlat / 2.0)))
    total = fields * nlon * cosine.sum()
    return np.sqrt(cosine) * total ** (-0.25)


def smooth_kernel(part, layers, edges, at_ref, factor_ref, x_ref, lon_ref, lat_ref, *rest):
    rows, nlon, snaps = x_ref.shape[1:]
    if edges:
        above_ref, below_ref, *out_refs = rest
    else:
        out_refs = rest
    inner = x_ref.shape[0] * (rows - 2)
    for j in range(layers):
        n = part * layers + (at_ref[0] ^ j)
        field, row = n // (rows - 2), 1 + n % (rows - 2)
        if edges:
            m = n - inner
            field = jnp.where(m < 0, field, m // 2)
            row = jnp.where(m < 0, row, (rows - 1) * (m % 2))
        up = x_ref[field, jnp.maximum(row - 1, 0)].astype(jnp.float32)
        down = x_ref[field, jnp.minimum(row + 1, rows - 1)].astype(jnp.float32)
        if edges:
            up = jnp.where(row == 0, above_ref[field, 0].astype(jnp.float32), up)
            down = jnp.where(row == rows - 1, below_ref[field, 0].astype(jnp.float32), down)
        x = x_ref[field, row].astype(jnp.float32)
        lon = jnp.broadcast_to(lon_ref[field, pl.ds(row, 1), :], (snaps, nlon)).T
        lat = jnp.broadcast_to(lat_ref[field, pl.ds(row, 1), :], (snaps, nlon)).T
        lon_part = pltpu.roll(x, 1, 0) + pltpu.roll(x, nlon - 1, 0) - 2.0 * x
        lat_part = up + down - 2.0 * x
        smooth = x + lon * lon_part + lat * lat_part
        out_refs[j][...] = (smooth * factor_ref[row]).astype(jnp.bfloat16)


def scaled_part(part, layers, at, factors, cells, lon_coeff, lat_coeff, halo):
    nlon, snaps = cells.shape[2:]
    vmem, smem = pl.BlockSpec(memory_space=pltpu.VMEM), pl.BlockSpec(memory_space=pltpu.SMEM)
    return pl.pallas_call(
        functools.partial(smooth_kernel, part, layers, bool(halo)),
        out_shape=[jax.ShapeDtypeStruct((nlon, snaps), jnp.bfloat16)] * layers,
        in_specs=[smem, smem] + [vmem] * (3 + len(halo)),
        out_specs=[vmem] * layers,
        compiler_params=pltpu.CompilerParams(vmem_limit_bytes=VMEM_BYTES),
        name="smooth_rows",
    )(at, factors, cells, lon_coeff, lat_coeff, *halo)


def product_kernel(layers, picks, last, at_ref, *refs):
    count = 4 * layers
    pieces, refs = refs[:count], refs[count:]
    if last:
        sum_ref, own_ref, out_ref, stack, right, sems = refs
    else:
        out_ref, stack, right, sems = refs
    depth, snaps = pieces[0].shape
    copies = [
        pltpu.make_async_copy(piece, stack.at[n // 2, pl.ds((n % 2) * depth, depth)], sems.at[n])
        for n, piece in enumerate(pieces)
    ]
    for copy in copies:
        copy.start()
    for copy in copies:
        copy.wait()
    for c in range(picks):
        right[:, c * snaps : (c + 1) * snaps] = stack[at_ref[c]]
    blocks = []
    for j in range(layers):
        product = lax.dot_general(
            stack[2 * j], right[...], (((0,), (0,)), ((), ())), preferred_element_type=jnp.float32
        )
        wide = out_ref.shape[2]
        for i in range(picks * snaps // wide):
            blocks.append(product[:, i * wide : (i + 1) * wide])
    if not last:
        for n, block in enumerate(blocks):
            out_ref[n] = block
        return
    blocks = [block + sum_ref[n] for n, block in enumerate(blocks)]
    own_ref[...] = blocks[0]
    largest = functools.reduce(jnp.maximum, [jnp.abs(block) for block in blocks[1:]])
    largest = jnp.maximum(jnp.max(largest, axis=(0, 1), keepdims=True), 1e-30)
    power = jnp.ceil(jnp.log2(largest)) - 15.0
    scale = jnp.exp2(-power)
    for n, block in enumerate(blocks[1:]):
        out_ref[n, :snaps] = block * scale
        out_ref[n, snaps:] = jnp.broadcast_to(power, (EXTRA, block.shape[1]))


def product_part(layers, columns, share, at, pieces, so_far):
    depth, snaps = pieces[0].shape
    picks, wide, count = columns * share, share * snaps, layers * columns
    vmem, smem = pl.BlockSpec(memory_space=pltpu.VMEM), pl.BlockSpec(memory_space=pltpu.SMEM)
    last = so_far is not None
    if last:
        out_shape = [
            jax.ShapeDtypeStruct((snaps, wide), jnp.float32),
            jax.ShapeDtypeStruct((count - 1, snaps + EXTRA, wide), jnp.float32),
        ]
    else:
        out_shape = [jax.ShapeDtypeStruct((count, snaps, wide), jnp.float32)]
    return pl.pallas_call(
        functools.partial(product_kernel, layers, picks, last),
        out_shape=out_shape,
        in_specs=[smem] + [pl.BlockSpec(memory_space=pl.ANY)] * len(pieces) + [vmem] * last,
        out_specs=[vmem] * len(out_shape),
        scratch_shapes=[
            pltpu.VMEM((2 * layers, 2 * depth, snaps), jnp.bfloat16),
            pltpu.VMEM((2 * depth, picks * snaps), jnp.bfloat16),
            pltpu.SemaphoreType.DMA((len(pieces),)),
        ],
        compiler_params=pltpu.CompilerParams(vmem_limit_bytes=VMEM_BYTES),
        name="block_products",
    )(at, *pieces, *([so_far] if last else []))


def shards(snapshots, lon_coeff, lat_coeff):
    snaps, fields, rows, nlon = snapshots.shape
    groups, bands = lax.axis_size("snap"), lax.axis_size("space")
    layers, columns, share = groups // 2, bands // 2, groups // bands
    me, band = lax.axis_index("snap"), lax.axis_index("space")
    layer, column, core = me // 2, band // 2, band % 2
    parts = fields * rows // layers
    inner_parts = fields * (rows - 2) // layers

    table = jnp.asarray(row_factors(bands * rows, fields, nlon), jnp.float32)
    factors = lax.dynamic_slice_in_dim(table, band * rows, rows)
    cells = jnp.transpose(snapshots, (1, 2, 3, 0))
    at = layer[None]
    scaled = [
        scaled_part(t, layers, at, factors, cells, lon_coeff, lat_coeff, ())
        for t in range(inner_parts)
    ]
    first = scaled[-1][0] if scaled else cells
    tail, head = after((cells[:, rows - 1 :], cells[:, :1]), first)
    ends = bands - 1
    halo = (
        lax.ppermute(tail, "space", [(i, i + 1) for i in range(ends)]),
        lax.ppermute(head, "space", [(i + 1, i) for i in range(ends)]),
    )
    scaled += [
        scaled_part(t, layers, at, factors, cells, lon_coeff, lat_coeff, halo)
        for t in range(inner_parts, parts)
    ]

    picked = [
        (((column ^ i) * 2 + core) * share + g) ^ me for i in range(columns) for g in range(share)
    ]
    picked = jnp.stack(picked).astype(jnp.int32)
    before, product = {}, None
    for t in range(parts):
        pieces = []
        for j in range(layers):
            held = scaled[t][j]
            if j:
                held = flip(after(held, before[j]) if j in before else held, "snap", 2 * j)
                before[j] = held
            other = flip(held, "snap", 1)
            pieces += [held, flip(held, "space", 1), other, flip(other, "space", 1)]
        if t < parts - 1 and product is None:
            (product,) = product_part(layers, columns, share, picked, pieces, None)
    if product is None:
        product = jnp.zeros((layers * columns, snaps, share * snaps), jnp.float32)
    own, blocks = product_part(layers, columns, share, picked, pieces, product)

    blocks = blocks.astype(jnp.float16)
    total = own
    for j in range(layers):
        for i in range(columns):
            if i or j:
                pairs = [
                    (s * bands + b, (s ^ (2 * j)) * bands + (b ^ (2 * i)))
                    for s in range(groups)
                    for b in range(bands)
                ]
                block = lax.ppermute(blocks[j * columns + i - 1], ("snap", "space"), pairs)
                block = block.astype(jnp.float32)
                total += block[:snaps] * jnp.exp2(block[snaps : snaps + 1])
    return total


def solution(mesh):
    return jax.shard_map(
        shards,
        mesh=mesh,
        in_specs=(P("snap", None, "space", None), P(None, "space", None), P(None, "space", None)),
        out_specs=P("snap", "space"),
        check_vma=False,
    )
```

```python
import functools
import math

import jax
import jax.numpy as jnp
import numpy as np
from jax import lax
from jax.experimental import pallas as pl
from jax.experimental.pallas import tpu as pltpu
from jax.sharding import PartitionSpec as P

EXTRA = 8
VMEM_BYTES = 16 * 2**20
ANY = pl.BlockSpec(memory_space=pl.ANY)
HBM = pl.BlockSpec(memory_space=pltpu.HBM)
VMEM = pl.BlockSpec(memory_space=pltpu.VMEM)
PARAMS = pltpu.CompilerParams(vmem_limit_bytes=VMEM_BYTES)


def flip(cells, axis, bits):
    count = lax.axis_size(axis)
    return lax.ppermute(cells, axis, [(i, i ^ bits) for i in range(count)])


def after(value, *earlier):
    return lax.optimization_barrier((value, *earlier))[0]


def row_factors(nlat, fields, nlon):
    cosine = np.cos(np.deg2rad(45.0 + 0.5 * (np.arange(nlat) + 0.5 - nlat / 2.0)))
    total = fields * nlon * cosine.sum()
    return [float(value) for value in np.sqrt(cosine) * total ** (-0.25)]


def chosen(values, at):
    value = jnp.float32(values[0])
    for n in range(1, len(values)):
        value = jnp.where(at == n, jnp.float32(values[n]), value)
    return value


def smooth_kernel(part, edges, factors, x_hbm, lon_hbm, lat_hbm, *rest):
    if edges:
        above_hbm, below_hbm, *rest = rest
    *out_refs, x_ref, lon_ref, lat_ref, above_ref, below_ref, sems = rest
    sources = [(lon_hbm, lon_ref), (lat_hbm, lat_ref), (x_hbm, x_ref)]
    if edges:
        sources += [(above_hbm, above_ref), (below_hbm, below_ref)]
    copies = [pltpu.make_async_copy(a, b, sems.at[n]) for n, (a, b) in enumerate(sources)]
    for copy in copies:
        copy.start()
    for copy in copies:
        copy.wait()
    rows, nlon, snaps = x_ref.shape[1:]
    if not edges:
        tail_ref, head_ref, *out_refs = out_refs
        tail_ref[...] = x_ref[:, rows - 1]
        head_ref[...] = x_ref[:, 0]
    layers = len(out_refs)
    layer, band = lax.axis_index("snap") // 2, lax.axis_index("space")
    inner = x_ref.shape[0] * (rows - 2)
    for j in reversed(range(layers)):
        n = part * layers + (layer ^ j)
        field, row = n // (rows - 2), 1 + n % (rows - 2)
        if edges:
            m = n - inner
            field = jnp.where(m < 0, field, m // 2)
            row = jnp.where(m < 0, row, (rows - 1) * (m % 2))
        up = x_ref[field, jnp.maximum(row - 1, 0)].astype(jnp.float32)
        down = x_ref[field, jnp.minimum(row + 1, rows - 1)].astype(jnp.float32)
        if edges:
            up = jnp.where(row == 0, above_ref[field].astype(jnp.float32), up)
            down = jnp.where(row == rows - 1, below_ref[field].astype(jnp.float32), down)
        x = x_ref[field, row].astype(jnp.float32)
        lon = jnp.broadcast_to(lon_ref[field, pl.ds(row, 1), :], (snaps, nlon)).T
        lat = jnp.broadcast_to(lat_ref[field, pl.ds(row, 1), :], (snaps, nlon)).T
        lon_part = pltpu.roll(x, 1, 0) + pltpu.roll(x, nlon - 1, 0) - 2.0 * x
        lat_part = up + down - 2.0 * x
        smooth = x + lon * lon_part + lat * lat_part
        factor = chosen(factors, band * rows + row)
        out_refs[j][...] = (smooth * factor).astype(jnp.bfloat16)


def scaled_part(part, layers, factors, cells, lon_coeff, lat_coeff, halo):
    fields, rows, nlon, snaps = cells.shape
    edge = (fields, nlon, snaps)
    row = jax.ShapeDtypeStruct((nlon, snaps), jnp.bfloat16)
    out_shape = [row] * layers
    in_place = [pltpu.with_memory_space_constraint(v, pltpu.HBM) for v in (cells, lon_coeff, lat_coeff)]
    if not halo:
        out_shape = [jax.ShapeDtypeStruct(edge, cells.dtype)] * 2 + out_shape
    return pl.pallas_call(
        functools.partial(smooth_kernel, part, bool(halo), factors),
        out_shape=out_shape,
        in_specs=[HBM] * 3 + [ANY] * len(halo),
        out_specs=[VMEM] * len(out_shape),
        scratch_shapes=[
            pltpu.VMEM(cells.shape, cells.dtype),
            pltpu.VMEM(lon_coeff.shape, lon_coeff.dtype),
            pltpu.VMEM(lat_coeff.shape, lat_coeff.dtype),
            pltpu.VMEM(edge, cells.dtype),
            pltpu.VMEM(edge, cells.dtype),
            pltpu.SemaphoreType.DMA((5,)),
        ],
        compiler_params=PARAMS,
        name="smooth_rows",
    )(*in_place, *halo)


def turn_kernel(*refs):
    *pieces, out_ref = refs
    snaps = pieces[0].shape[1]
    at = [lax.broadcasted_iota(jnp.int32, (snaps, snaps), axis) for axis in (0, 1)]
    one = jnp.where(at[0] == at[1], 1.0, 0.0).astype(jnp.bfloat16)
    for n, piece in enumerate(pieces):
        turned = lax.dot_general(
            one, piece[...], (((1,), (1,)), ((), ())), preferred_element_type=jnp.float32
        )
        out_ref[n // 2, n % 2] = turned.astype(jnp.bfloat16)


def turned(pieces):
    depth, snaps = pieces[0].shape
    return pl.pallas_call(
        turn_kernel,
        out_shape=jax.ShapeDtypeStruct((len(pieces) // 2, 2, snaps, depth), jnp.bfloat16),
        in_specs=[VMEM] * len(pieces),
        out_specs=VMEM,
        compiler_params=PARAMS,
        name="turn_pieces",
    )(*pieces)


def product_kernel(layers, columns, share, last, left_ref, *refs):
    count, picks = 4 * layers, columns * share
    pieces, refs = refs[:count], refs[count:]
    if last:
        sum_ref, own_ref, out_ref, right, sems = refs
    else:
        out_ref, right, sems = refs
    depth, snaps = pieces[0].shape
    me, band = lax.axis_index("snap"), lax.axis_index("space")
    for i in range(columns):
        for g in range(share):
            c = i * share + g
            wanted = ((((band // 2) ^ i) * 2 + band % 2) * share + g) ^ me
            for n, piece in enumerate(pieces):

                @pl.when(wanted == n // 2)
                def _():
                    pltpu.make_async_copy(
                        piece, right.at[n % 2, :, pl.ds(c * snaps, snaps)], sems.at[c, n % 2]
                    ).start()

    for c in range(picks):
        for side in range(2):
            pltpu.make_async_copy(
                pieces[side], right.at[side, :, pl.ds(c * snaps, snaps)], sems.at[c, side]
            ).wait()
    blocks, wide = [], out_ref.shape[2]
    for j in range(layers):
        product = sum(
            jnp.dot(left_ref[j, side], right[side], preferred_element_type=jnp.float32)
            for side in range(2)
        )
        for i in range(columns):
            blocks.append(product[:, i * wide : (i + 1) * wide])
    if not last:
        for n, block in enumerate(blocks):
            out_ref[n] = block
        return
    blocks = [block + sum_ref[n] for n, block in enumerate(blocks)]
    own_ref[...] = blocks[0]
    largest = functools.reduce(jnp.maximum, [jnp.abs(block) for block in blocks[1:]])
    largest = jnp.maximum(jnp.max(largest, axis=(0, 1), keepdims=True), 1e-30)
    power = jnp.ceil(jnp.log2(largest)) - 15.0
    scale = jnp.exp2(-power)
    for n, block in enumerate(blocks[1:]):
        out_ref[n, :snaps] = block * scale
        out_ref[n, snaps:] = jnp.broadcast_to(power, (EXTRA, block.shape[1]))


def product_part(layers, columns, share, left, pieces, so_far):
    depth, snaps = pieces[0].shape
    picks, wide, count = columns * share, share * snaps, layers * columns
    last = so_far is not None
    if last:
        out_shape = [
            jax.ShapeDtypeStruct((snaps, wide), jnp.float32),
            jax.ShapeDtypeStruct((count - 1, snaps + EXTRA, wide), jnp.float32),
        ]
    else:
        out_shape = [jax.ShapeDtypeStruct((count, snaps, wide), jnp.float32)]
    return pl.pallas_call(
        functools.partial(product_kernel, layers, columns, share, last),
        out_shape=out_shape,
        in_specs=[VMEM] + [ANY] * len(pieces) + [VMEM] * last,
        out_specs=[VMEM] * len(out_shape),
        scratch_shapes=[
            pltpu.VMEM((2, depth, picks * snaps), jnp.bfloat16),
            pltpu.SemaphoreType.DMA((picks, 2)),
        ],
        compiler_params=PARAMS,
        name="block_products",
    )(left, *pieces, *([so_far] if last else []))


def shards(snapshots, lon_coeff, lat_coeff):
    snaps, fields, rows, nlon = snapshots.shape
    groups, bands = lax.axis_size("snap"), lax.axis_size("space")
    layers, columns, share = groups // 2, bands // 2, groups // bands
    parts = fields * rows // layers
    inner_parts = fields * (rows - 2) // layers

    factors = row_factors(bands * rows, fields, nlon)
    cells = jnp.transpose(snapshots, (1, 2, 3, 0))
    tail, head = cells[:, rows - 1], cells[:, 0]
    scaled = []
    for t in range(inner_parts):
        tail, head, *part = scaled_part(t, layers, factors, cells, lon_coeff, lat_coeff, ())
        scaled.append(part)
    if scaled:
        tail, head = after((tail, head), flip(scaled[0][0], "space", 1))
    ends = bands - 1
    halo = (
        lax.ppermute(tail, "space", [(i, i + 1) for i in range(ends)]),
        lax.ppermute(head, "space", [(i + 1, i) for i in range(ends)]),
    )
    scaled += [
        scaled_part(t, layers, factors, cells, lon_coeff, lat_coeff, halo)
        for t in range(inner_parts, parts)
    ]
    ready = scaled[-1][0]

    far = range(layers // 2, layers)
    near = range(1, layers // 2)
    own = [after(scaled[t][0], ready) for t in range(parts)]
    held = [{0: own[t]} for t in range(parts)]
    other = [{0: flip(own[t], "snap", 1)} for t in range(parts)]
    begun = [other[t][0] for t in range(parts)]
    for t in range(parts):
        for j in near:
            held[t][j] = after(flip(scaled[t][j], "snap", 2 * j), ready, *begun)
            other[t][j] = flip(held[t][j], "snap", 1)
    for t in range(parts):
        for j in far:
            held[t][j] = after(flip(scaled[t][j], "snap", 2 * j), ready, *begun)
            other[t][j] = flip(held[t][j], "snap", 1)
        begun = [other[t][j] for j in far]
    final = [held[parts - 1][j] for j in far]
    product = None
    for t in range(parts):
        rows_of, pieces = [], []
        for j in range(layers):
            mine, theirs = held[t][j], other[t][j]
            mine_too = flip(after(mine, *final), "space", 1)
            theirs_too = flip(after(theirs, *final), "space", 1)
            rows_of += [mine, mine_too]
            pieces += [mine, mine_too, theirs, theirs_too]
        left = turned(rows_of)
        if t < parts - 1 and product is None:
            (product,) = product_part(layers, columns, share, left, pieces, None)
    if product is None:
        product = jnp.zeros((layers * columns, snaps, share * snaps), jnp.float32)
    own, blocks = product_part(layers, columns, share, left, pieces, product)

    blocks = blocks.astype(jnp.float16)
    total = own
    for j in range(layers):
        for i in range(columns):
            if i or j:
                pairs = [
                    (s * bands + b, (s ^ (2 * j)) * bands + (b ^ (2 * i)))
                    for s in range(groups)
                    for b in range(bands)
                ]
                block = lax.ppermute(blocks[j * columns + i - 1], ("snap", "space"), pairs)
                block = block.astype(jnp.float32)
                total += block[:snaps] * jnp.exp2(block[snaps : snaps + 1])
    return total


def solution(mesh):
    return jax.shard_map(
        shards,
        mesh=mesh,
        in_specs=(P("snap", None, "space", None), P(None, "space", None), P(None, "space", None)),
        out_specs=P("snap", "space"),
        check_vma=False,
    )
```

```python
import functools
import math

import jax
import jax.numpy as jnp
import numpy as np
from jax import lax
from jax.experimental import pallas as pl
from jax.experimental.pallas import tpu as pltpu
from jax.sharding import PartitionSpec as P

EXTRA = 8
VMEM_BYTES = 16 * 2**20
ANY = pl.BlockSpec(memory_space=pl.ANY)
HBM = pl.BlockSpec(memory_space=pltpu.HBM)
VMEM = pl.BlockSpec(memory_space=pltpu.VMEM)
UNIT = 18 * 10**8
QUICK = pl.CostEstimate(flops=1, bytes_accessed=1, transcendentals=0)
PARAMS = pltpu.CompilerParams(vmem_limit_bytes=VMEM_BYTES)


def flip(cells, axis, bits):
    count = lax.axis_size(axis)
    return lax.ppermute(cells, axis, [(i, i ^ bits) for i in range(count)])


def after(value, *earlier):
    return lax.optimization_barrier((value, *earlier))[0]


def row_factors(nlat, fields, nlon):
    cosine = np.cos(np.deg2rad(45.0 + 0.5 * (np.arange(nlat) + 0.5 - nlat / 2.0)))
    total = fields * nlon * cosine.sum()
    return [float(value) for value in np.sqrt(cosine) * total ** (-0.25)]


def chosen(values, at):
    value = jnp.float32(values[0])
    for n in range(1, len(values)):
        value = jnp.where(at == n, jnp.float32(values[n]), value)
    return value


def smooth_kernel(part, layers, edges, factors, x_hbm, lon_hbm, lat_hbm, *rest):
    if edges:
        inside_hbm, outside_hbm, *rest = rest
    *out_refs, x_ref, lon_ref, lat_ref, inside_ref, outside_ref, sems = rest
    sources = [(lon_hbm, lon_ref), (lat_hbm, lat_ref), (x_hbm, x_ref)]
    if edges:
        sources += [(inside_hbm, inside_ref), (outside_hbm, outside_ref)]
    copies = [pltpu.make_async_copy(a, b, sems.at[n]) for n, (a, b) in enumerate(sources)]
    for copy in copies:
        copy.start()
    for copy in copies:
        copy.wait()
    rows, nlon, snaps = x_ref.shape[1:]
    layer, band = lax.axis_index("snap") // 2, lax.axis_index("space")
    upper = band % 2 == 0
    inner = x_ref.shape[0] * (rows - 2)
    for j in reversed(range(layers)):
        n = part * layers + (layer ^ j)
        field, row = n // (rows - 2), 1 + n % (rows - 2)
        if edges:
            m = n - inner
            field = jnp.where(m < 0, field, m // 2)
            row = jnp.where(m < 0, row, (rows - 1) * (m % 2))
        up = x_ref[field, jnp.maximum(row - 1, 0)].astype(jnp.float32)
        down = x_ref[field, jnp.minimum(row + 1, rows - 1)].astype(jnp.float32)
        if edges:
            inside = inside_ref[field].astype(jnp.float32)
            outside = outside_ref[field].astype(jnp.float32)
            up = jnp.where(row == 0, jnp.where(upper, outside, inside), up)
            down = jnp.where(row == rows - 1, jnp.where(upper, inside, outside), down)
        x = x_ref[field, row].astype(jnp.float32)
        lon = jnp.broadcast_to(lon_ref[field, pl.ds(row, 1), :], (snaps, nlon)).T
        lat = jnp.broadcast_to(lat_ref[field, pl.ds(row, 1), :], (snaps, nlon)).T
        lon_part = pltpu.roll(x, 1, 0) + pltpu.roll(x, nlon - 1, 0) - 2.0 * x
        lat_part = up + down - 2.0 * x
        smooth = x + lon * lon_part + lat * lat_part
        factor = chosen(factors, band * rows + row)
        out_refs[j][...] = (smooth * factor).astype(jnp.bfloat16)


def scaled_part(part, layers, factors, cells, lon_coeff, lat_coeff, halo):
    fields, rows, nlon, snaps = cells.shape
    edge = (fields, nlon, snaps)
    out_shape = [jax.ShapeDtypeStruct((nlon, snaps), jnp.bfloat16)] * layers
    in_place = [pltpu.with_memory_space_constraint(v, pltpu.HBM) for v in (cells, lon_coeff, lat_coeff)]
    return pl.pallas_call(
        functools.partial(smooth_kernel, part, layers, bool(halo), factors),
        out_shape=out_shape,
        in_specs=[HBM] * 3 + [ANY] * len(halo),
        out_specs=[VMEM] * len(out_shape),
        scratch_shapes=[
            pltpu.VMEM(cells.shape, cells.dtype),
            pltpu.VMEM(lon_coeff.shape, lon_coeff.dtype),
            pltpu.VMEM(lat_coeff.shape, lat_coeff.dtype),
            pltpu.VMEM(edge, cells.dtype),
            pltpu.VMEM(edge, cells.dtype),
            pltpu.SemaphoreType.DMA((5,)),
        ],
        compiler_params=PARAMS,
        cost_estimate=QUICK,
        name="smooth_rows",
    )(*in_place, *halo)


def edges_kernel(x_hbm, inside_ref, outside_ref, sems):
    rows = x_hbm.shape[1]
    upper = lax.axis_index("space") % 2 == 0
    copies = [
        pltpu.make_async_copy(x_hbm.at[:, jnp.where(upper, a, b)], out_ref, sems.at[n])
        for n, (a, b, out_ref) in enumerate(
            [(rows - 1, 0, inside_ref), (0, rows - 1, outside_ref)]
        )
    ]
    for copy in copies:
        copy.start()
    for copy in copies:
        copy.wait()


def edges_of(cells):
    fields, _, nlon, snaps = cells.shape
    edge = jax.ShapeDtypeStruct((fields, nlon, snaps), cells.dtype)
    return pl.pallas_call(
        edges_kernel,
        out_shape=[edge, edge],
        in_specs=[HBM],
        out_specs=[VMEM, VMEM],
        scratch_shapes=[pltpu.SemaphoreType.DMA((2,))],
        compiler_params=PARAMS,
        cost_estimate=QUICK,
        name="band_edges",
    )(pltpu.with_memory_space_constraint(cells, pltpu.HBM))


def join_kernel(*refs):
    *pieces, out_ref = refs
    depth = pieces[0].shape[0]
    for n, piece in enumerate(pieces):
        out_ref[n * depth : (n + 1) * depth] = piece[...]


def join(pieces, cost=0.0):
    depth, snaps = pieces[0].shape
    return pl.pallas_call(
        join_kernel,
        out_shape=jax.ShapeDtypeStruct((len(pieces) * depth, snaps), jnp.bfloat16),
        in_specs=[VMEM] * len(pieces),
        out_specs=VMEM,
        compiler_params=PARAMS,
        cost_estimate=pl.CostEstimate(
            flops=1 + int(cost * UNIT), bytes_accessed=1, transcendentals=0
        ),
        name="join_pieces",
    )(*pieces)


def turn_kernel(places, depth, *refs):
    *arrays, out_ref = refs
    snaps = arrays[0].shape[1]
    at = [lax.broadcasted_iota(jnp.int32, (snaps, snaps), axis) for axis in (0, 1)]
    one = jnp.where(at[0] == at[1], 1.0, 0.0).astype(jnp.bfloat16)
    for n, (array, row) in enumerate(places):
        for side in range(2):
            piece = arrays[2 * array + side][pl.ds(row, depth)]
            turned = lax.dot_general(
                one, piece, (((1,), (1,)), ((), ())), preferred_element_type=jnp.float32
            )
            out_ref[n, side] = turned.astype(jnp.bfloat16)


def turned(arrays, places, depth):
    snaps = arrays[0].shape[1]
    return pl.pallas_call(
        functools.partial(turn_kernel, places, depth),
        out_shape=jax.ShapeDtypeStruct((len(places), 2, snaps, depth), jnp.bfloat16),
        in_specs=[VMEM] * len(arrays),
        out_specs=VMEM,
        compiler_params=PARAMS,
        cost_estimate=QUICK,
        name="turn_pieces",
    )(*arrays)


def product_kernel(layers, columns, share, places, *refs):
    parts = len(places)
    lefts, refs = refs[:parts], refs[parts:]
    *arrays, own_ref, out_ref, right, sems = refs
    depth, snaps = right.shape[2], arrays[0].shape[1]
    me, band = lax.axis_index("snap"), lax.axis_index("space")
    picks = columns * share
    for t in range(parts):
        for c in range(picks):
            i, g = c // share, c % share
            wanted = ((band ^ (2 * i)) * share + g) ^ me
            for j, (array, row) in enumerate(places[t]):
                for y in range(2):

                    @pl.when(wanted == 2 * j + y)
                    def _():
                        for side in range(2):
                            pltpu.make_async_copy(
                                arrays[4 * array + 2 * y + side].at[pl.ds(row, depth)],
                                right.at[t, side, :, pl.ds(c * snaps, snaps)],
                                sems.at[t, c, side],
                            ).start()

    for t in range(parts):
        for c in range(picks):
            for side in range(2):
                pltpu.make_async_copy(
                    arrays[0].at[pl.ds(0, depth)],
                    right.at[t, side, :, pl.ds(c * snaps, snaps)],
                    sems.at[t, c, side],
                ).wait()
    blocks, wide = [], share * snaps
    for j in range(layers):
        product = sum(
            jnp.dot(lefts[t][j, side], right[t, side], preferred_element_type=jnp.float32)
            for t in range(parts)
            for side in range(2)
        )
        for i in range(columns):
            blocks.append(product[:, i * wide : (i + 1) * wide])
    own_ref[...] = blocks[0]
    largest = functools.reduce(jnp.maximum, [jnp.abs(block) for block in blocks[1:]])
    largest = jnp.maximum(jnp.max(largest, axis=(0, 1), keepdims=True), 1e-30)
    power = jnp.ceil(jnp.log2(largest)) - 15.0
    scale = jnp.exp2(-power)
    for n, block in enumerate(blocks[1:]):
        out_ref[n, :snaps] = block * scale
        out_ref[n, snaps:] = jnp.broadcast_to(power, (EXTRA, block.shape[1]))


def block_products(layers, columns, share, lefts, arrays, places):
    parts = len(lefts)
    snaps, depth = lefts[0].shape[2:]
    wide = snaps * share
    return pl.pallas_call(
        functools.partial(product_kernel, layers, columns, share, places),
        out_shape=[
            jax.ShapeDtypeStruct((snaps, wide), jnp.float32),
            jax.ShapeDtypeStruct((layers * columns - 1, snaps + EXTRA, wide), jnp.float32),
        ],
        in_specs=[VMEM] * parts + [ANY] * len(arrays),
        out_specs=[VMEM, VMEM],
        scratch_shapes=[
            pltpu.VMEM((parts, 2, depth, columns * wide), jnp.bfloat16),
            pltpu.SemaphoreType.DMA((parts, columns * share, 2)),
        ],
        compiler_params=PARAMS,
        cost_estimate=QUICK,
        name="block_products",
    )(*lefts, *arrays)


def shards(snapshots, lon_coeff, lat_coeff):
    snaps, fields, rows, nlon = snapshots.shape
    groups, bands = lax.axis_size("snap"), lax.axis_size("space")
    layers, columns, share = groups // 2, bands // 2, groups // bands
    parts = fields * rows // layers
    inner_parts = fields * (rows - 2) // layers

    factors = row_factors(bands * rows, fields, nlon)
    cells = jnp.transpose(snapshots, (1, 2, 3, 0))
    inside, outside = edges_of(cells)
    scaled = [
        scaled_part(t, layers, factors, cells, lon_coeff, lat_coeff, ())
        for t in range(inner_parts)
    ]
    steps = [(i, i + 1) for i in range(1, bands - 1, 2)]
    halo = (
        flip(inside, "space", 1),
        lax.ppermute(outside, "space", steps + [(i, j) for j, i in steps]),
    )
    count = layers // 2
    scaled += [
        scaled_part(t, layers, factors, cells, lon_coeff, lat_coeff, halo)
        for t in range(inner_parts, parts)
    ]

    spans = [[(t, 0) for t in range(parts)]]
    own = join([scaled[t][0] for t in range(parts)])
    own_other = flip(own, "snap", 1)
    held, other = [own], [own_other]
    for j in range(1, count):
        near = flip(join([scaled[t][j] for t in range(parts)]), "snap", 2 * j)
        held.append(near)
        other.append(join([flip(near, "snap", 1)], 2.5))
        spans.append([(t, j) for t in range(parts)])
    before = own_other
    for t in range(parts):
        last = t == parts - 1
        far = [flip(scaled[t][j], "snap", 2 * j) for j in range(count, layers)]
        far = join(far, 1.9 if last else 1.3)
        sent = flip(after(far, before), "snap", 1)
        held.append(far)
        other.append(join([sent], 3.0) if last else sent)
        spans.append([(t, j) for j in range(count, layers)])
        before = before if last else sent
    late = [held[-1], before]
    held_too = [flip(after(array, *late), "space", 1) for array in held]
    places, lefts = [], []
    for t in range(parts):
        at = [(n, span) for n, span in enumerate(spans) if (t, span[-1][1]) in span]
        where = [(n, span.index((t, j)) * nlon) for j in range(layers) for n, span in at if (t, j) in span]
        places.append(where)
        used = [n for n, _ in at]
        arrays = [array for n in used for array in (held[n], held_too[n])]
        lefts.append(turned(arrays, [(used.index(n), row) for n, row in where], nlon))
    other_too = [flip(after(array, *late), "space", 1) for array in other[:-1]]
    other_too.append(flip(after(other[-1], *lefts), "space", 1))
    arrays = [array for arrays in zip(held, held_too, other, other_too) for array in arrays]
    total, blocks = block_products(layers, columns, share, lefts, arrays, places)

    blocks = blocks.astype(jnp.float16)
    order = [(j, i) for j in range(layers) for i in range(columns) if i or j]
    for j, i in sorted(order, key=lambda at: ((at[0] + at[1]) % 2, -(at[0] or layers - 1.5))):
        pairs = [
            (s * bands + b, (s ^ (2 * j)) * bands + (b ^ (2 * i)))
            for s in range(groups)
            for b in range(bands)
        ]
        block = lax.ppermute(blocks[j * columns + i - 1], ("snap", "space"), pairs)
        block = block.astype(jnp.float32)
        total += block[:snaps] * jnp.exp2(block[snaps : snaps + 1])
    return total


def solution(mesh):
    return jax.shard_map(
        shards,
        mesh=mesh,
        in_specs=(P("snap", None, "space", None), P(None, "space", None), P(None, "space", None)),
        out_specs=P("snap", "space"),
        check_vma=False,
    )
```

```python
import functools
import math

import jax
import jax.numpy as jnp
import numpy as np
from jax import lax
from jax.experimental import pallas as pl
from jax.experimental.pallas import tpu as pltpu
from jax.sharding import PartitionSpec as P

EXTRA = 8
VMEM_BYTES = 16 * 2**20
ANY = pl.BlockSpec(memory_space=pl.ANY)
HBM = pl.BlockSpec(memory_space=pltpu.HBM)
VMEM = pl.BlockSpec(memory_space=pltpu.VMEM)
FAR, FAR_LAST, NEAR_OTHER, FAR_OTHER, FAR_LAST_OTHER = 1.1, 2.2, 4.0, 0.5, 3.0
UNIT = 18 * 10**8
QUICK = pl.CostEstimate(flops=1, bytes_accessed=1, transcendentals=0)
PARAMS = pltpu.CompilerParams(vmem_limit_bytes=VMEM_BYTES)


def flip(cells, axis, bits):
    count = lax.axis_size(axis)
    return lax.ppermute(cells, axis, [(i, i ^ bits) for i in range(count)])


def after(value, *earlier):
    return lax.optimization_barrier((value, *earlier))[0]


def row_factors(nlat, fields, nlon):
    cosine = np.cos(np.deg2rad(45.0 + 0.5 * (np.arange(nlat) + 0.5 - nlat / 2.0)))
    total = fields * nlon * cosine.sum()
    return [float(value) for value in np.sqrt(cosine) * total ** (-0.25)]


def chosen(values, at):
    value = jnp.float32(values[0])
    for n in range(1, len(values)):
        value = jnp.where(at == n, jnp.float32(values[n]), value)
    return value


def smooth_kernel(part, layers, edges, factors, x_hbm, lon_hbm, lat_hbm, *rest):
    if edges:
        inside_hbm, outside_hbm, *rest = rest
    *out_refs, x_ref, lon_ref, lat_ref, inside_ref, outside_ref, sems = rest
    sources = [(lon_hbm, lon_ref), (lat_hbm, lat_ref), (x_hbm, x_ref)]
    if edges:
        sources += [(inside_hbm, inside_ref), (outside_hbm, outside_ref)]
    copies = [pltpu.make_async_copy(a, b, sems.at[n]) for n, (a, b) in enumerate(sources)]
    for copy in copies:
        copy.start()
    for copy in copies:
        copy.wait()
    rows, nlon, snaps = x_ref.shape[1:]
    layer, band = lax.axis_index("snap") // 2, lax.axis_index("space")
    upper = band % 2 == 0
    inner = x_ref.shape[0] * (rows - 2)
    for j in reversed(range(layers)):
        n = part * layers + (layer ^ j)
        field, row = n // (rows - 2), 1 + n % (rows - 2)
        if edges:
            m = n - inner
            field = jnp.where(m < 0, field, m // 2)
            row = jnp.where(m < 0, row, (rows - 1) * (m % 2))
        up = x_ref[field, jnp.maximum(row - 1, 0)].astype(jnp.float32)
        down = x_ref[field, jnp.minimum(row + 1, rows - 1)].astype(jnp.float32)
        if edges:
            inside = inside_ref[field].astype(jnp.float32)
            outside = outside_ref[field].astype(jnp.float32)
            up = jnp.where(row == 0, jnp.where(upper, outside, inside), up)
            down = jnp.where(row == rows - 1, jnp.where(upper, inside, outside), down)
        x = x_ref[field, row].astype(jnp.float32)
        lon = jnp.broadcast_to(lon_ref[field, pl.ds(row, 1), :], (snaps, nlon)).T
        lat = jnp.broadcast_to(lat_ref[field, pl.ds(row, 1), :], (snaps, nlon)).T
        lon_part = pltpu.roll(x, 1, 0) + pltpu.roll(x, nlon - 1, 0) - 2.0 * x
        lat_part = up + down - 2.0 * x
        smooth = x + lon * lon_part + lat * lat_part
        factor = chosen(factors, band * rows + row)
        out_refs[j][...] = (smooth * factor).astype(jnp.bfloat16)


def scaled_part(part, layers, factors, cells, lon_coeff, lat_coeff, halo):
    fields, rows, nlon, snaps = cells.shape
    edge = (fields, nlon, snaps)
    out_shape = [jax.ShapeDtypeStruct((nlon, snaps), jnp.bfloat16)] * layers
    in_place = [pltpu.with_memory_space_constraint(v, pltpu.HBM) for v in (cells, lon_coeff, lat_coeff)]
    return pl.pallas_call(
        functools.partial(smooth_kernel, part, layers, bool(halo), factors),
        out_shape=out_shape,
        in_specs=[HBM] * 3 + [ANY] * len(halo),
        out_specs=[VMEM] * len(out_shape),
        scratch_shapes=[
            pltpu.VMEM(cells.shape, cells.dtype),
            pltpu.VMEM(lon_coeff.shape, lon_coeff.dtype),
            pltpu.VMEM(lat_coeff.shape, lat_coeff.dtype),
            pltpu.VMEM(edge, cells.dtype),
            pltpu.VMEM(edge, cells.dtype),
            pltpu.SemaphoreType.DMA((5,)),
        ],
        compiler_params=PARAMS,
        cost_estimate=QUICK,
        name="smooth_rows",
    )(*in_place, *halo)


def edges_kernel(x_hbm, inside_ref, outside_ref, sems):
    rows = x_hbm.shape[1]
    upper = lax.axis_index("space") % 2 == 0
    copies = [
        pltpu.make_async_copy(x_hbm.at[:, jnp.where(upper, a, b)], out_ref, sems.at[n])
        for n, (a, b, out_ref) in enumerate(
            [(rows - 1, 0, inside_ref), (0, rows - 1, outside_ref)]
        )
    ]
    for copy in copies:
        copy.start()
    for copy in copies:
        copy.wait()


def edges_of(cells):
    fields, _, nlon, snaps = cells.shape
    edge = jax.ShapeDtypeStruct((fields, nlon, snaps), cells.dtype)
    return pl.pallas_call(
        edges_kernel,
        out_shape=[edge, edge],
        in_specs=[HBM],
        out_specs=[VMEM, VMEM],
        scratch_shapes=[pltpu.SemaphoreType.DMA((2,))],
        compiler_params=PARAMS,
        cost_estimate=QUICK,
        name="band_edges",
    )(pltpu.with_memory_space_constraint(cells, pltpu.HBM))


def join_kernel(*refs):
    *pieces, out_ref = refs
    depth = pieces[0].shape[0]
    for n, piece in enumerate(pieces):
        out_ref[n * depth : (n + 1) * depth] = piece[...]


def join(pieces, cost=0.0):
    depth, snaps = pieces[0].shape
    return pl.pallas_call(
        join_kernel,
        out_shape=jax.ShapeDtypeStruct((len(pieces) * depth, snaps), jnp.bfloat16),
        in_specs=[VMEM] * len(pieces),
        out_specs=VMEM,
        compiler_params=PARAMS,
        cost_estimate=pl.CostEstimate(
            flops=1 + int(cost * UNIT), bytes_accessed=1, transcendentals=0
        ),
        name="join_pieces",
    )(*pieces)


def turn_kernel(places, depth, *refs):
    *arrays, out_ref = refs
    snaps = arrays[0].shape[1]
    at = [lax.broadcasted_iota(jnp.int32, (snaps, snaps), axis) for axis in (0, 1)]
    one = jnp.where(at[0] == at[1], 1.0, 0.0).astype(jnp.bfloat16)
    for n, (array, row) in enumerate(places):
        for side in range(2):
            piece = arrays[2 * array + side][pl.ds(row, depth)]
            turned = lax.dot_general(
                one, piece, (((1,), (1,)), ((), ())), preferred_element_type=jnp.float32
            )
            out_ref[n, side] = turned.astype(jnp.bfloat16)


def turned(arrays, places, depth):
    snaps = arrays[0].shape[1]
    return pl.pallas_call(
        functools.partial(turn_kernel, places, depth),
        out_shape=jax.ShapeDtypeStruct((len(places), 2, snaps, depth), jnp.bfloat16),
        in_specs=[VMEM] * len(arrays),
        out_specs=VMEM,
        compiler_params=PARAMS,
        cost_estimate=QUICK,
        name="turn_pieces",
    )(*arrays)


def product_kernel(layers, columns, share, places, *refs):
    parts = len(places)
    lefts, refs = refs[:parts], refs[parts:]
    *arrays, own_ref, out_ref, right = refs
    depth, snaps = right.shape[2], arrays[0].shape[1]
    me, band = lax.axis_index("snap"), lax.axis_index("space")
    picks = columns * share
    for t in range(parts):
        for c in range(picks):
            i, g = c // share, c % share
            wanted = ((band ^ (2 * i)) * share + g) ^ me
            for j, (array, row) in enumerate(places[t]):
                for y in range(2):

                    @pl.when(wanted == 2 * j + y)
                    def _():
                        for side in range(2):
                            piece = arrays[4 * array + 2 * y + side][pl.ds(row, depth)]
                            right[t, side, :, c * snaps : (c + 1) * snaps] = piece

    product = sum(
        jnp.dot(
            lefts[t][:, side].reshape(layers * snaps, depth),
            right[t, side],
            preferred_element_type=jnp.float32,
        )
        for t in range(parts)
        for side in range(2)
    )
    wide = share * snaps
    blocks = [
        product[j * snaps : (j + 1) * snaps, i * wide : (i + 1) * wide]
        for j in range(layers)
        for i in range(columns)
    ]
    own_ref[...] = blocks[0]
    largest = functools.reduce(jnp.maximum, [jnp.abs(block) for block in blocks[1:]])
    largest = jnp.maximum(jnp.max(largest, axis=(0, 1), keepdims=True), 1e-30)
    power = jnp.ceil(jnp.log2(largest)) - 15.0
    scale = jnp.exp2(-power)
    for n, block in enumerate(blocks[1:]):
        out_ref[n, :snaps] = block * scale
        out_ref[n, snaps:] = jnp.broadcast_to(power, (EXTRA, block.shape[1]))


def block_products(layers, columns, share, lefts, arrays, places):
    parts = len(lefts)
    snaps, depth = lefts[0].shape[2:]
    wide = snaps * share
    return pl.pallas_call(
        functools.partial(product_kernel, layers, columns, share, places),
        out_shape=[
            jax.ShapeDtypeStruct((snaps, wide), jnp.float32),
            jax.ShapeDtypeStruct((layers * columns - 1, snaps + EXTRA, wide), jnp.float32),
        ],
        in_specs=[VMEM] * (parts + len(arrays)),
        out_specs=[VMEM, VMEM],
        scratch_shapes=[
            pltpu.VMEM((parts, 2, depth, columns * wide), jnp.bfloat16),
        ],
        compiler_params=PARAMS,
        cost_estimate=QUICK,
        name="block_products",
    )(*lefts, *arrays)


def shards(snapshots, lon_coeff, lat_coeff):
    snaps, fields, rows, nlon = snapshots.shape
    groups, bands = lax.axis_size("snap"), lax.axis_size("space")
    layers, columns, share = groups // 2, bands // 2, groups // bands
    parts = fields * rows // layers
    inner_parts = fields * (rows - 2) // layers

    factors = row_factors(bands * rows, fields, nlon)
    cells = jnp.transpose(snapshots, (1, 2, 3, 0))
    inside, outside = edges_of(cells)
    scaled = [
        scaled_part(t, layers, factors, cells, lon_coeff, lat_coeff, ())
        for t in range(inner_parts)
    ]
    steps = [(i, i + 1) for i in range(1, bands - 1, 2)]
    halo = (
        flip(inside, "space", 1),
        lax.ppermute(outside, "space", steps + [(i, j) for j, i in steps]),
    )
    count = layers // 2
    scaled += [
        scaled_part(t, layers, factors, cells, lon_coeff, lat_coeff, halo)
        for t in range(inner_parts, parts)
    ]

    spans = [[(t, 0) for t in range(parts)]]
    own = join([scaled[t][0] for t in range(parts)])
    own_other = flip(own, "snap", 1)
    held, other = [own], [own_other]
    for j in range(1, count):
        near = flip(join([scaled[t][j] for t in range(parts)]), "snap", 2 * j)
        held.append(near)
        other.append(join([flip(near, "snap", 1)], NEAR_OTHER))
        spans.append([(t, j) for t in range(parts)])
    before = own_other
    for t in range(parts):
        last = t == parts - 1
        far = [flip(scaled[t][j], "snap", 2 * j) for j in range(count, layers)]
        far = join(far, FAR_LAST if last else FAR)
        sent = flip(after(far, before), "snap", 1)
        held.append(far)
        other.append(join([sent], FAR_LAST_OTHER if last else FAR_OTHER))
        spans.append([(t, j) for j in range(count, layers)])
        before = before if last else sent
    late = [held[-1], before]
    held_too = [flip(after(array, *late), "space", 1) for array in held]
    places, lefts = [], []
    for t in range(parts):
        at = [(n, span) for n, span in enumerate(spans) if (t, span[-1][1]) in span]
        where = [(n, span.index((t, j)) * nlon) for j in range(layers) for n, span in at if (t, j) in span]
        places.append(where)
        used = [n for n, _ in at]
        arrays = [array for n in used for array in (held[n], held_too[n])]
        lefts.append(turned(arrays, [(used.index(n), row) for n, row in where], nlon))
    other_too = [flip(after(array, *late), "space", 1) for array in other[:-1]]
    other_too.append(flip(after(other[-1], *lefts), "space", 1))
    arrays = [array for arrays in zip(held, held_too, other, other_too) for array in arrays]
    total, blocks = block_products(layers, columns, share, lefts, arrays, places)

    blocks = blocks.astype(jnp.float16)
    order = [(j, i) for j in range(layers) for i in range(columns) if i or j]
    for j, i in sorted(order, key=lambda at: (1, (at[0] + 1) % layers) if sum(at) % 2 else (0, -at[0])):
        pairs = [
            (s * bands + b, (s ^ (2 * j)) * bands + (b ^ (2 * i)))
            for s in range(groups)
            for b in range(bands)
        ]
        block = lax.ppermute(blocks[j * columns + i - 1], ("snap", "space"), pairs)
        block = block.astype(jnp.float32)
        total += block[:snaps] * jnp.exp2(block[snaps : snaps + 1])
    return total


def solution(mesh):
    return jax.shard_map(
        shards,
        mesh=mesh,
        in_specs=(P("snap", None, "space", None), P(None, "space", None), P(None, "space", None)),
        out_specs=P("snap", "space"),
        check_vma=False,
    )
```

```python
import functools
import math

import jax
import jax.numpy as jnp
import numpy as np
from jax import lax
from jax.experimental import pallas as pl
from jax.experimental.pallas import tpu as pltpu
from jax.sharding import PartitionSpec as P

EXTRA = 8
VMEM_BYTES = 16 * 2**20
ANY = pl.BlockSpec(memory_space=pl.ANY)
HBM = pl.BlockSpec(memory_space=pltpu.HBM)
VMEM = pl.BlockSpec(memory_space=pltpu.VMEM)
FAR, FAR_LAST, NEAR_OTHER, FAR_OTHER, FAR_LAST_OTHER = 1.1, 2.2, 4.0, 0.5, 3.6
UNIT = 18 * 10**8
QUICK = pl.CostEstimate(flops=1, bytes_accessed=1, transcendentals=0)
PARAMS = pltpu.CompilerParams(vmem_limit_bytes=VMEM_BYTES)


def flip(cells, axis, bits):
    count = lax.axis_size(axis)
    return lax.ppermute(cells, axis, [(i, i ^ bits) for i in range(count)])


def after(value, *earlier):
    return lax.optimization_barrier((value, *earlier))[0]


def row_factors(nlat, fields, nlon):
    cosine = np.cos(np.deg2rad(45.0 + 0.5 * (np.arange(nlat) + 0.5 - nlat / 2.0)))
    total = fields * nlon * cosine.sum()
    return [float(value) for value in np.sqrt(cosine) * total ** (-0.25)]


def chosen(values, at):
    value = jnp.float32(values[0])
    for n in range(1, len(values)):
        value = jnp.where(at == n, jnp.float32(values[n]), value)
    return value


def smooth_kernel(part, layers, edges, factors, x_hbm, lon_hbm, lat_hbm, *rest):
    if edges:
        inside_hbm, outside_hbm, *rest = rest
    *out_refs, x_ref, lon_ref, lat_ref, inside_ref, outside_ref, sems = rest
    sources = [(lon_hbm, lon_ref), (lat_hbm, lat_ref), (x_hbm, x_ref)]
    if edges:
        sources += [(inside_hbm, inside_ref), (outside_hbm, outside_ref)]
    copies = [pltpu.make_async_copy(a, b, sems.at[n]) for n, (a, b) in enumerate(sources)]
    for copy in copies:
        copy.start()
    for copy in copies:
        copy.wait()
    rows, nlon, snaps = x_ref.shape[1:]
    layer, band = lax.axis_index("snap") // 2, lax.axis_index("space")
    upper = band % 2 == 0
    inner = x_ref.shape[0] * (rows - 2)
    for j in reversed(range(layers)):
        n = part * layers + (layer ^ j)
        field, row = n // (rows - 2), 1 + n % (rows - 2)
        if edges:
            m = n - inner
            field = jnp.where(m < 0, field, m // 2)
            row = jnp.where(m < 0, row, (rows - 1) * (m % 2))
        up = x_ref[field, jnp.maximum(row - 1, 0)].astype(jnp.float32)
        down = x_ref[field, jnp.minimum(row + 1, rows - 1)].astype(jnp.float32)
        if edges:
            inside = inside_ref[field].astype(jnp.float32)
            outside = outside_ref[field].astype(jnp.float32)
            up = jnp.where(row == 0, jnp.where(upper, outside, inside), up)
            down = jnp.where(row == rows - 1, jnp.where(upper, inside, outside), down)
        x = x_ref[field, row].astype(jnp.float32)
        lon = jnp.broadcast_to(lon_ref[field, pl.ds(row, 1), :], (snaps, nlon)).T
        lat = jnp.broadcast_to(lat_ref[field, pl.ds(row, 1), :], (snaps, nlon)).T
        lon_part = pltpu.roll(x, 1, 0) + pltpu.roll(x, nlon - 1, 0) - 2.0 * x
        lat_part = up + down - 2.0 * x
        smooth = x + lon * lon_part + lat * lat_part
        factor = chosen(factors, band * rows + row)
        out_refs[j][...] = (smooth * factor).astype(jnp.bfloat16)


def scaled_part(part, layers, factors, cells, lon_coeff, lat_coeff, halo):
    fields, rows, nlon, snaps = cells.shape
    edge = (fields, nlon, snaps)
    out_shape = [jax.ShapeDtypeStruct((nlon, snaps), jnp.bfloat16)] * layers
    in_place = [pltpu.with_memory_space_constraint(v, pltpu.HBM) for v in (cells, lon_coeff, lat_coeff)]
    return pl.pallas_call(
        functools.partial(smooth_kernel, part, layers, bool(halo), factors),
        out_shape=out_shape,
        in_specs=[HBM] * 3 + [ANY] * len(halo),
        out_specs=[VMEM] * len(out_shape),
        scratch_shapes=[
            pltpu.VMEM(cells.shape, cells.dtype),
            pltpu.VMEM(lon_coeff.shape, lon_coeff.dtype),
            pltpu.VMEM(lat_coeff.shape, lat_coeff.dtype),
            pltpu.VMEM(edge, cells.dtype),
            pltpu.VMEM(edge, cells.dtype),
            pltpu.SemaphoreType.DMA((5,)),
        ],
        compiler_params=PARAMS,
        cost_estimate=QUICK,
        name="smooth_rows",
    )(*in_place, *halo)


def edges_kernel(x_hbm, inside_ref, outside_ref, sems):
    rows = x_hbm.shape[1]
    upper = lax.axis_index("space") % 2 == 0
    copies = [
        pltpu.make_async_copy(x_hbm.at[:, jnp.where(upper, a, b)], out_ref, sems.at[n])
        for n, (a, b, out_ref) in enumerate(
            [(rows - 1, 0, inside_ref), (0, rows - 1, outside_ref)]
        )
    ]
    for copy in copies:
        copy.start()
    for copy in copies:
        copy.wait()


def edges_of(cells):
    fields, _, nlon, snaps = cells.shape
    edge = jax.ShapeDtypeStruct((fields, nlon, snaps), cells.dtype)
    return pl.pallas_call(
        edges_kernel,
        out_shape=[edge, edge],
        in_specs=[HBM],
        out_specs=[VMEM, VMEM],
        scratch_shapes=[pltpu.SemaphoreType.DMA((2,))],
        compiler_params=PARAMS,
        cost_estimate=QUICK,
        name="band_edges",
    )(pltpu.with_memory_space_constraint(cells, pltpu.HBM))


def join_kernel(*refs):
    *pieces, out_ref = refs
    depth = pieces[0].shape[0]
    for n, piece in enumerate(pieces):
        out_ref[n * depth : (n + 1) * depth] = piece[...]


def join(pieces, cost=0.0):
    depth, snaps = pieces[0].shape
    return pl.pallas_call(
        join_kernel,
        out_shape=jax.ShapeDtypeStruct((len(pieces) * depth, snaps), jnp.bfloat16),
        in_specs=[VMEM] * len(pieces),
        out_specs=VMEM,
        compiler_params=PARAMS,
        cost_estimate=pl.CostEstimate(
            flops=1 + int(cost * UNIT), bytes_accessed=1, transcendentals=0
        ),
        name="join_pieces",
    )(*pieces)


def turn_kernel(places, depth, *refs):
    *arrays, out_ref = refs
    snaps = arrays[0].shape[1]
    at = [lax.broadcasted_iota(jnp.int32, (snaps, snaps), axis) for axis in (0, 1)]
    one = jnp.where(at[0] == at[1], 1.0, 0.0).astype(jnp.bfloat16)
    for n, (array, row) in enumerate(places):
        for side in range(2):
            piece = arrays[2 * array + side][pl.ds(row, depth)]
            turned = lax.dot_general(
                one, piece, (((1,), (1,)), ((), ())), preferred_element_type=jnp.float32
            )
            out_ref[n, side] = turned.astype(jnp.bfloat16)


def turned(arrays, places, depth):
    snaps = arrays[0].shape[1]
    return pl.pallas_call(
        functools.partial(turn_kernel, places, depth),
        out_shape=jax.ShapeDtypeStruct((len(places), 2, snaps, depth), jnp.bfloat16),
        in_specs=[VMEM] * len(arrays),
        out_specs=VMEM,
        compiler_params=PARAMS,
        cost_estimate=QUICK,
        name="turn_pieces",
    )(*arrays)


def product_kernel(layers, columns, share, places, *refs):
    parts = len(places)
    near_ref, *far_refs = refs[: 1 + parts]
    refs = refs[1 + parts :]
    *arrays, own_ref, out_ref, right = refs
    depth, snaps = right.shape[2], arrays[0].shape[1]
    me, band = lax.axis_index("snap"), lax.axis_index("space")
    picks = columns * share
    for t in range(parts):
        for c in range(picks):
            i, g = c // share, c % share
            wanted = ((band ^ (2 * i)) * share + g) ^ me
            for j, (array, row) in enumerate(places[t]):
                for y in range(2):

                    @pl.when(wanted == 2 * j + y)
                    def _():
                        for side in range(2):
                            piece = arrays[4 * array + 2 * y + side][pl.ds(row, depth)]
                            right[t, side, :, c * snaps : (c + 1) * snaps] = piece

    near = near_ref.shape[0] // parts
    product = sum(
        jnp.dot(
            jnp.concatenate(
                [near_ref[t * near : (t + 1) * near, side], far_refs[t][:, side]], axis=0
            ).reshape(layers * snaps, depth),
            right[t, side],
            preferred_element_type=jnp.float32,
        )
        for t in range(parts)
        for side in range(2)
    )
    wide = share * snaps
    blocks = [
        product[j * snaps : (j + 1) * snaps, i * wide : (i + 1) * wide]
        for j in range(layers)
        for i in range(columns)
    ]
    own_ref[...] = blocks[0]
    largest = functools.reduce(jnp.maximum, [jnp.abs(block) for block in blocks[1:]])
    largest = jnp.maximum(jnp.max(largest, axis=(0, 1), keepdims=True), 1e-30)
    power = jnp.ceil(jnp.log2(largest)) - 15.0
    scale = jnp.exp2(-power)
    for n, block in enumerate(blocks[1:]):
        out_ref[n, :snaps] = block * scale
        out_ref[n, snaps:] = jnp.broadcast_to(power, (EXTRA, block.shape[1]))


def block_products(layers, columns, share, lefts, arrays, places):
    parts = len(places)
    snaps, depth = lefts[0].shape[2:]
    wide = snaps * share
    return pl.pallas_call(
        functools.partial(product_kernel, layers, columns, share, places),
        out_shape=[
            jax.ShapeDtypeStruct((snaps, wide), jnp.float32),
            jax.ShapeDtypeStruct((layers * columns - 1, snaps + EXTRA, wide), jnp.float32),
        ],
        in_specs=[VMEM] * (1 + parts + len(arrays)),
        out_specs=[VMEM, VMEM],
        scratch_shapes=[
            pltpu.VMEM((parts, 2, depth, columns * wide), jnp.bfloat16),
        ],
        compiler_params=PARAMS,
        cost_estimate=QUICK,
        name="block_products",
    )(*lefts, *arrays)


def shards(snapshots, lon_coeff, lat_coeff):
    snaps, fields, rows, nlon = snapshots.shape
    groups, bands = lax.axis_size("snap"), lax.axis_size("space")
    layers, columns, share = groups // 2, bands // 2, groups // bands
    parts = fields * rows // layers
    inner_parts = fields * (rows - 2) // layers

    factors = row_factors(bands * rows, fields, nlon)
    cells = jnp.transpose(snapshots, (1, 2, 3, 0))
    inside, outside = edges_of(cells)
    scaled = [
        scaled_part(t, layers, factors, cells, lon_coeff, lat_coeff, ())
        for t in range(inner_parts)
    ]
    steps = [(i, i + 1) for i in range(1, bands - 1, 2)]
    halo = (
        flip(inside, "space", 1),
        lax.ppermute(outside, "space", steps + [(i, j) for j, i in steps]),
    )
    count = layers // 2
    scaled += [
        scaled_part(t, layers, factors, cells, lon_coeff, lat_coeff, halo)
        for t in range(inner_parts, parts)
    ]

    own = join([scaled[t][0] for t in range(parts)])
    own_other = flip(own, "snap", 1)
    held, other = [own], [own_other]
    for j in range(1, count):
        near = flip(join([scaled[t][j] for t in range(parts)]), "snap", 2 * j)
        held.append(near)
        other.append(join([flip(near, "snap", 1)], NEAR_OTHER))
    before = own_other
    for t in range(parts):
        last = t == parts - 1
        far = [flip(scaled[t][j], "snap", 2 * j) for j in range(count, layers)]
        far = join(far, FAR_LAST if last else FAR)
        sent = flip(after(far, before), "snap", 1)
        held.append(far)
        other.append(join([sent], FAR_LAST_OTHER if last else FAR_OTHER))
        before = before if last else sent
    late = [held[-1], before]
    held_too = [flip(after(array, *late), "space", 1) for array in held]
    places = [
        [(j, t * nlon) for j in range(count)] + [(count + t, n * nlon) for n in range(layers - count)]
        for t in range(parts)
    ]
    arrays = [array for pair in zip(held[:count], held_too) for array in pair]
    lefts = [turned(arrays, [at for t in range(parts) for at in places[t][:count]], nlon)]
    for t in range(parts):
        arrays = [held[count + t], held_too[count + t]]
        lefts.append(turned(arrays, [(0, n * nlon) for n in range(layers - count)], nlon))
    other_too = [flip(after(array, *late), "space", 1) for array in other[:-1]]
    other_too.append(flip(after(other[-1], *lefts), "space", 1))
    arrays = [array for arrays in zip(held, held_too, other, other_too) for array in arrays]
    total, blocks = block_products(layers, columns, share, lefts, arrays, places)

    blocks = blocks.astype(jnp.float16)
    order = [(j, i) for j in range(layers) for i in range(columns) if i or j]
    for j, i in sorted(order, key=lambda at: (1, (at[0] + 1) % layers) if sum(at) % 2 else (0, -at[0])):
        pairs = [
            (s * bands + b, (s ^ (2 * j)) * bands + (b ^ (2 * i)))
            for s in range(groups)
            for b in range(bands)
        ]
        block = lax.ppermute(blocks[j * columns + i - 1], ("snap", "space"), pairs)
        block = block.astype(jnp.float32)
        total += block[:snaps] * jnp.exp2(block[snaps : snaps + 1])
    return total


def solution(mesh):
    return jax.shard_map(
        shards,
        mesh=mesh,
        in_specs=(P("snap", None, "space", None), P(None, "space", None), P(None, "space", None)),
        out_specs=P("snap", "space"),
        check_vma=False,
    )
```
